128 devices in a mesh: row: 8 (over y, x_hi), col: 16 (over x_lo, z, core).
Axes of the slice: x: 4 (x_hi: 2, x_lo: 2; x = x_hi * 2 + x_lo), y: 4, z: 4, core: 2. Of those that a mesh axis runs over, the one named last changes fastest.
Arguments:
- start_block: float32 [32, 49152], P(None, ('row', 'col')), may hold values from -6 to 6
- center: float32 [1], replicated, may hold values from 1.05 to 1.15
- half_width: float32 [1], replicated, may hold values from 0.85 to 0.95
- matrix_tiles: bfloat16 [8, 768, 192, 192], P('row', 'col')
- tile_row: int32 [8, 768], P('row', 'col'), may hold values from 0 to 31, as said below
- tile_col: int32 [8, 768], P('row', 'col'), may hold values from 0 to 15, as said below
- tile_live: int32 [8, 768], P('row', 'col'), may hold values from 0 to 1
Outputs:
- filtered: float32 [32, 49152], P(None, ('row', 'col'))
- previous: float32 [32, 49152], P(None, ('row', 'col'))
The draws below stay inside these ranges and needn't reach their ends.
Inputs may be any that keep to these rules, and one draw needn't show every extreme that they name: tile_row lies within the device's row clusters; on a live slot the block row's atom order is at most the block column's. tile_col lies within the device's column clusters.
All inputs are finite; a program needn't handle non-finite values.
Results may differ from the reference program's by a relative error of at most 0.03.
Values may be sent and summed in bfloat16 or wider, within the bound.
No kernel may reach another device: no remote copies, remote signals or barrier semaphores. Data moves between devices by JAX's collectives and lax.ppermute only.
A program may use at most 64 MiB of HBM per device.

```python
import math
import jax
import jax.numpy as jnp
from jax import lax

B = 192
K = 32
DEG = 8
CL_DEV = 2
SLOTS = 48
NC = 256
N = 49152
N_ROW = 8
N_COL = 16


def pattern(key):
    panel_cols = CL_DEV * N_ROW
    factor = N_COL // N_ROW
    band_reach = max(2, SLOTS // (CL_DEV * N_COL))
    shape_all = (N_ROW, N_COL * SLOTS)
    row_grid = jnp.broadcast_to(jnp.arange(N_ROW, dtype=jnp.int32)[:, None], shape_all)
    flat_slot = jnp.broadcast_to(jnp.arange(N_COL * SLOTS, dtype=jnp.int32)[None, :], shape_all)
    col_grid = flat_slot // SLOTS
    slot_index = flat_slot % SLOTS
    base = jax.random.fold_in(key, 11)
    key_col, key_sub, key_step, key_live = jax.random.split(base, 4)
    col_local = jax.random.randint(key_col, shape_all, 0, panel_cols, dtype=jnp.int32)
    sub_row = jax.random.randint(key_sub, shape_all, 0, factor, dtype=jnp.int32)
    step_back = jax.random.randint(key_step, shape_all, 0, band_reach, dtype=jnp.int32)
    coin = jax.random.randint(key_live, shape_all, 0, 4, dtype=jnp.int32)
    row_block = row_grid * factor + sub_row
    row_local = col_local - step_back
    broken = (row_local < 0) | (step_back == 0) & (row_block > col_grid)
    diagonal = (col_grid // factor == row_grid) & (slot_index < panel_cols)
    col_local = jnp.where(diagonal, slot_index, col_local)
    sub_row = jnp.where(diagonal, col_grid - row_grid * factor, sub_row)
    row_local = jnp.where(diagonal, slot_index, jnp.clip(row_local, 0, panel_cols - 1))
    live = jnp.where(diagonal | ~broken & (coin > 0), 1, 0).astype(jnp.int32)
    row_ids = (sub_row * panel_cols + row_local).astype(jnp.int32)
    return (row_ids, col_local.astype(jnp.int32), live, diagonal)


def draw_tile_row(key, part):
    shared = pattern(key)
    return shared[0]


def draw_tile_col(key, part):
    shared = pattern(key)
    return shared[1]


def draw_tile_live(key, part):
    shared = pattern(key)
    return shared[2]


def draw_matrix_tiles(key, part):
    shared = pattern(key)
    key = jax.random.fold_in(key, 5)
    scale = 0.45 / math.sqrt(1.2 * SLOTS * B / CL_DEV)
    shape_all = (N_ROW, N_COL * SLOTS, B, B)
    noise = jax.random.normal(key, shape_all, jnp.float32) * scale
    identity = jnp.eye(B, dtype=jnp.float32)
    shift = shared[3].astype(jnp.float32)[:, :, None, None] * 0.5 * identity[None, None, :, :]
    return (noise + shift).astype(jnp.bfloat16)


def level_of(key, extent, cuts, smallest, top_value):
    level, own = 1.0, jax.random.fold_in(key, 6)
    for dim, parts in cuts:
        heights = jnp.exp(jax.random.uniform(jax.random.fold_in(own, dim), (parts,), jnp.float32, smallest / len(cuts), top_value / len(cuts)))
        level = level * jnp.repeat(heights, extent[dim] // parts).reshape([-1 if axis == dim else 1 for axis in range(len(extent))])
    return level


def gaussian(key, extent, scale, limit, cuts=(), kind=jnp.bfloat16):
    drawn = scale * jax.random.normal(key, extent, jnp.float32)
    if cuts:
        drawn = drawn * level_of(key, extent, cuts, -0.22, 0.18)
    return jnp.clip(drawn, -limit, limit).astype(kind)


def setup_inputs(seed: int = 0) -> dict:
    splits = jax.random.split(jax.random.key(seed), 8)
    start_block = gaussian(splits[0], (K, N), 1.0, 6.0, ((1, 128),), jnp.float32)
    center = jnp.clip(jax.random.uniform(splits[1], (1,), jnp.float32, 1.05, 1.15), 1.05, 1.15)
    half_width = jnp.clip(jax.random.uniform(splits[2], (1,), jnp.float32, 0.85, 0.95), 0.85, 0.95)
    matrix_tiles = draw_matrix_tiles(jax.random.fold_in(splits[7], 71), 0)
    tile_row = draw_tile_row(jax.random.fold_in(splits[7], 71), 0)
    tile_col = draw_tile_col(jax.random.fold_in(splits[7], 71), 0)
    tile_live = draw_tile_live(jax.random.fold_in(splits[7], 71), 0)
    return {"start_block": start_block, "center": center, "half_width": half_width, "matrix_tiles": matrix_tiles, "tile_row": tile_row, "tile_col": tile_col, "tile_live": tile_live}


def apply_matrix(row_vectors, matrix_tiles, tile_row, tile_col, tile_live):
    panel_rows = CL_DEV * N_COL
    panel_cols = CL_DEV * N_ROW
    zero_index = jnp.zeros((), jnp.int32)

    def visit(totals, device):
        row_index = (device // N_COL).astype(jnp.int32)
        col_index = (device % N_COL).astype(jnp.int32)
        slot_start = (col_index * SLOTS).astype(jnp.int32)
        stored = lax.dynamic_slice(matrix_tiles, (row_index, slot_start, zero_index, zero_index), (1, SLOTS, B, B))[0].astype(jnp.float32)
        row_ids = lax.dynamic_slice(tile_row, (row_index, slot_start), (1, SLOTS))[0] + row_index * panel_rows
        col_ids = lax.dynamic_slice(tile_col, (row_index, slot_start), (1, SLOTS))[0] + col_index * panel_cols
        weights = lax.dynamic_slice(tile_live, (row_index, slot_start), (1, SLOTS))[0].astype(jnp.float32)
        row_ids = row_ids.astype(jnp.int32)
        col_ids = col_ids.astype(jnp.int32)
        x_col = row_vectors[:, col_ids, :]
        x_row = row_vectors[:, row_ids, :]
        direct = jnp.einsum("ksb,sab->ksa", x_col, stored, precision=lax.Precision.HIGHEST) * weights[None, :, None]
        mirrored = jnp.einsum("ksa,sab->ksb", x_row, stored, precision=lax.Precision.HIGHEST) * weights[None, :, None]
        totals = totals.at[:, row_ids, :].add(direct)
        totals = totals.at[:, col_ids, :].add(mirrored)
        return totals, None

    start = jnp.zeros(row_vectors.shape, jnp.float32)
    totals, _ = lax.scan(visit, start, jnp.arange(N_ROW * N_COL, dtype=jnp.int32))
    return totals


def advance(degree, product, current, earlier, center_value, half_value):
    if degree == 0:
        return (product - center_value * current) / half_value
    return 2.0 * (product - center_value * current) / half_value - earlier


def reference(start_block, center, half_width, matrix_tiles, tile_row, tile_col, tile_live):
    current = start_block.reshape(K, NC, B)
    earlier = current
    for degree in range(DEG):
        rounded = current.astype(jnp.bfloat16).astype(jnp.float32)
        product = apply_matrix(rounded, matrix_tiles, tile_row, tile_col, tile_live)
        following = advance(degree, product, current, earlier, center[0], half_width[0])
        earlier, current = current, following
    return current.reshape(K, N), earlier.reshape(K, N)
```

```python
import jax
import jax.numpy as jnp
from jax import lax
from jax.experimental import pallas as pl
from jax.experimental.pallas import tpu as pltpu
from jax.sharding import PartitionSpec as P

DEG = 8
GROUP = 8


def products_kernel(table, x_ref, own_ref, other_ref, out_ref, x_wide, total):
    clusters, vectors, _ = x_wide.shape
    size = own_ref.shape[-1]
    pairs = clusters // 2
    low = lax.broadcasted_iota(jnp.int32, (vectors, 128), 1) < 64

    for pair in range(pairs):
        first, middle, last = (x_ref[pair, :, 128 * i : 128 * (i + 1)].astype(jnp.float32) for i in range(3))
        middle_rolled, last_rolled = pltpu.roll(middle, 64, 1), pltpu.roll(last, 64, 1)
        x_wide[2 * pair, :, :128] = first.astype(jnp.bfloat16)
        x_wide[2 * pair, :, 128:] = middle.astype(jnp.bfloat16)
        x_wide[2 * pair + 1, :, :128] = jnp.where(low, middle_rolled, last_rolled).astype(jnp.bfloat16)
        x_wide[2 * pair + 1, :, 128:] = last_rolled.astype(jnp.bfloat16)

    total[...] = jnp.zeros_like(total)

    def run(contract):
        for part, tiles in enumerate((own_ref, other_ref)):

            @pl.loop(0, table[0, 1 + part])
            def _(group):
                sums = [
                    lax.dot_general(
                        x_wide[table[3 + part, group * GROUP + member], :, :size],
                        tiles[table[1 + part, group * GROUP + member]],
                        (((1,), (contract,)), ((), ())),
                        preferred_element_type=jnp.float32,
                    )
                    for member in range(GROUP)
                ]
                for member in range(GROUP):
                    where = table[5 + part, group * GROUP + member]
                    total[where, :, :size] += sums[member]

    @pl.when(table[0, 0] == 0)
    def _():
        run(0)

    @pl.when(table[0, 0] == 1)
    def _():
        run(1)

    for pair in range(pairs):
        even_a, even_b = total[2 * pair, :, :128], total[2 * pair, :, 128:]
        odd_a = pltpu.roll(total[2 * pair + 1, :, :128], 64, 1)
        odd_b = pltpu.roll(total[2 * pair + 1, :, 128:], 64, 1)
        out_ref[pair, :, :128] = even_a.astype(jnp.bfloat16)
        out_ref[pair, :, 128:256] = jnp.where(low, even_b, odd_a).astype(jnp.bfloat16)
        out_ref[pair, :, 256:] = jnp.where(low, odd_a, odd_b).astype(jnp.bfloat16)


def products(table, x, own, other):
    pairs, vectors, width = x.shape
    count, size, _ = own.shape
    smem = pl.BlockSpec(memory_space=pltpu.SMEM)
    vmem = pl.BlockSpec(memory_space=pltpu.VMEM)
    flops = 2 * 2 * count * size * size * vectors
    return pl.pallas_call(
        products_kernel,
        out_shape=jax.ShapeDtypeStruct(x.shape, jnp.bfloat16),
        in_specs=[smem, vmem, vmem, vmem],
        out_specs=vmem,
        scratch_shapes=[
            pltpu.VMEM((2 * pairs, vectors, 256), jnp.bfloat16),
            pltpu.VMEM((2 * pairs + 1, vectors, 256), jnp.float32),
        ],
        compiler_params=pltpu.CompilerParams(vmem_limit_bytes=24 * 1024 * 1024),
        cost_estimate=pl.CostEstimate(flops=flops, bytes_accessed=2 * count * size * size * 2, transcendentals=0),
    )(table, x, own, other)


def body(start_block, center, half_width, matrix_tiles, tile_row, tile_col, tile_live):
    vectors, width = start_block.shape
    slots_here = tile_row.shape[1]
    row_count, col_count = lax.axis_size("row"), lax.axis_size("col")
    side = row_count
    core = lax.axis_index("col") % 2
    axes = ("row", "col")

    def device(r, c2, h):
        return r * col_count + 2 * c2 + h

    grid = [(r, c2, h) for r in range(side) for c2 in range(side) for h in range(2)]
    swap = [(device(r, c2, h), device(r, c2, 1 - h)) for r, c2, h in grid]
    turn = [(device(r, c2, h), device(c2, r, h)) for r, c2, h in grid]
    along_row = [[[device(r, k, h) for k in range(side)] for r in range(side)] for h in range(2)]
    along_col = [[[device(k, c2, h) for k in range(side)] for c2 in range(side)] for h in range(2)]
    gather_groups = along_row[0] + along_col[1]
    scatter_groups = along_col[0] + along_row[1]

    def exchange(value, groups):
        return lax.all_to_all(value, axes, 0, 0, axis_index_groups=groups, tiled=False)

    own = matrix_tiles[0]
    other = lax.ppermute(own, axes, swap)
    panel = 2 * side
    col_here = tile_col[0] + core * panel
    ids = jnp.stack([tile_row[0], col_here, tile_live[0]])
    ids = jnp.stack([ids, lax.ppermute(ids, axes, swap)], 1)
    alive = ids[2] > 0
    position = jnp.cumsum(alive.astype(jnp.int32), axis=1) - 1
    places = slots_here + GROUP
    hit = (position[:, None, :] == jnp.arange(places)[None, :, None]) & alive[:, None, :]
    counts = jnp.sum(alive.astype(jnp.int32), axis=1)

    def pick(value, empty):
        found = jnp.sum(jnp.where(hit, value[:, None, :], 0), axis=2)
        return jnp.where(jnp.arange(places)[None, :] < counts[:, None], found, empty).astype(jnp.int32)

    slots = pick(jnp.broadcast_to(jnp.arange(slots_here)[None, :], alive.shape), 0)
    ins = pick(jnp.where(core == 0, ids[0], ids[1]), 0)
    outs = pick(jnp.where(core == 0, ids[1], ids[0]), 4 * side)
    info = jnp.concatenate([core[None], (counts + GROUP - 1) // GROUP]).astype(jnp.int32)
    table = jnp.concatenate([jnp.pad(info, (0, places - 3))[None], slots, ins, outs])

    mine = start_block
    theirs = lax.ppermute(mine, axes, swap)
    by_row = jnp.where(core == 0, jnp.stack([mine, theirs]), jnp.stack([theirs, mine]))
    current = jnp.where(core == 0, by_row, lax.ppermute(by_row, axes, turn))
    earlier = current
    center_value, half_value = center[0], half_width[0]
    for degree in range(DEG):
        rounded = current.astype(jnp.bfloat16)
        x = exchange(jnp.broadcast_to(rounded[None], (side, *rounded.shape)), gather_groups)
        partial = products(table, x.reshape(2 * side, vectors, width), own, other)
        parts = exchange(partial.reshape(side, 2, vectors, width), scatter_groups)
        share = jnp.sum(parts.astype(jnp.float32), axis=0).astype(jnp.bfloat16)
        product = lax.ppermute(share, axes, swap).astype(jnp.float32) + lax.ppermute(share, axes, turn).astype(jnp.float32)
        following = (product - center_value * current) / half_value
        if degree > 0:
            following = 2.0 * following - earlier
        earlier, current = current, following

    def own_pair(value):
        sent = lax.ppermute(value[1], axes, swap)
        return jnp.where(core == 0, value[0], sent)

    return own_pair(current), own_pair(earlier)


def solution(mesh):
    in_specs = (
        P(None, ("row", "col")),
        P(),
        P(),
        P("row", "col", None, None),
        P("row", "col"),
        P("row", "col"),
        P("row", "col"),
    )
    out_specs = (P(None, ("row", "col")), P(None, ("row", "col")))
    return jax.shard_map(body, mesh=mesh, in_specs=in_specs, out_specs=out_specs, check_vma=False)
```

```python
import jax
import jax.numpy as jnp
from jax import lax
from jax.experimental import pallas as pl
from jax.experimental.pallas import tpu as pltpu
from jax.sharding import PartitionSpec as P

DEG = 8
GROUP = 8


def keep_kernel(own_ref, other_ref, kept_ref, sems):
    count = own_ref.shape[0]
    copies = [
        pltpu.make_async_copy(ref, kept_ref.at[pl.ds(part * count, count)], sems.at[part])
        for part, ref in enumerate((own_ref, other_ref))
    ]
    for copy in copies:
        copy.start()
    for copy in copies:
        copy.wait()


def keep(own, other):
    count, size, _ = own.shape
    any_space = pl.BlockSpec(memory_space=pl.ANY)
    return pl.pallas_call(
        keep_kernel,
        out_shape=jax.ShapeDtypeStruct((2 * count, size, size), own.dtype),
        in_specs=[any_space, any_space],
        out_specs=pl.BlockSpec(memory_space=pltpu.VMEM),
        scratch_shapes=[pltpu.SemaphoreType.DMA((2,))],
        compiler_params=pltpu.CompilerParams(vmem_limit_bytes=16 * 1024 * 1024),
        cost_estimate=pl.CostEstimate(flops=0, bytes_accessed=4 * count * size * size * 2, transcendentals=0),
    )(own, other)


def products_kernel(table, fold_ref, x_ref, tiles_ref, out_ref, x_wide, total):
    vectors, size = x_wide.shape[1], tiles_ref.shape[-1]
    pairs = x_ref.shape[0]
    low = lax.broadcasted_iota(jnp.int32, (vectors, 128), 1) < 64
    fold = fold_ref[:1, :]

    def place(cluster, half, value):
        x_wide[cluster, :, 128 * half : 128 * (half + 1)] = value.astype(jnp.bfloat16)
        total[cluster, :, 128 * half : 128 * (half + 1)] = value * fold

    for pair in range(pairs):
        first, middle, last = (x_ref[pair, :, 128 * i : 128 * (i + 1)].astype(jnp.float32) for i in range(3))
        middle_rolled, last_rolled = pltpu.roll(middle, 64, 1), pltpu.roll(last, 64, 1)
        place(2 * pair, 0, first)
        place(2 * pair, 1, middle)
        place(2 * pair + 1, 0, jnp.where(low, middle_rolled, last_rolled))
        place(2 * pair + 1, 1, last_rolled)
    for half in range(2):
        place(2 * pairs, half, jnp.zeros((vectors, 128), jnp.float32))

    def run(contract):
        @pl.loop(0, table[0, 1])
        def _(group):
            sums = [
                lax.dot_general(
                    x_wide[table[2, group * GROUP + member], :, :size],
                    tiles_ref[table[1, group * GROUP + member]],
                    (((1,), (contract,)), ((), ())),
                    preferred_element_type=jnp.float32,
                )
                for member in range(GROUP)
            ]
            for member in range(GROUP):
                total[table[3, group * GROUP + member], :, :size] += sums[member]

    @pl.when(table[0, 0] == 0)
    def _():
        run(0)

    @pl.when(table[0, 0] == 1)
    def _():
        run(1)

    for pair in range(pairs):
        even_a, even_b = total[2 * pair, :, :128], total[2 * pair, :, 128:]
        odd_a = pltpu.roll(total[2 * pair + 1, :, :128], 64, 1)
        odd_b = pltpu.roll(total[2 * pair + 1, :, 128:], 64, 1)
        out_ref[pair, :, :128] = even_a.astype(jnp.bfloat16)
        out_ref[pair, :, 128:256] = jnp.where(low, even_b, odd_a).astype(jnp.bfloat16)
        out_ref[pair, :, 256:] = jnp.where(low, odd_a, odd_b).astype(jnp.bfloat16)


def products(table, fold, x, tiles):
    pairs, vectors, width = x.shape
    count, size, _ = tiles.shape
    vmem = pl.BlockSpec(memory_space=pltpu.VMEM)
    return pl.pallas_call(
        products_kernel,
        out_shape=jax.ShapeDtypeStruct(x.shape, jnp.bfloat16),
        in_specs=[pl.BlockSpec(memory_space=pltpu.SMEM), vmem, vmem, vmem],
        out_specs=vmem,
        scratch_shapes=[
            pltpu.VMEM((2 * pairs + 1, vectors, 256), jnp.bfloat16),
            pltpu.VMEM((2 * pairs + 1, vectors, 256), jnp.float32),
        ],
        compiler_params=pltpu.CompilerParams(vmem_limit_bytes=16 * 1024 * 1024),
        cost_estimate=pl.CostEstimate(
            flops=2 * count * size * size * vectors, bytes_accessed=count * size * size * 2, transcendentals=0
        ),
    )(table, fold, x, tiles)


def column_owner(side):
    def ring(a, b, n):
        return min((a - b) % n, (b - a) % n)

    half = side // 2
    owner = []
    for s in range(side):
        away = sorted(range(side), key=lambda k: (ring(k % half, s % half, half) + (k // half != s // half), k))
        near = sorted(range(side), key=lambda q: (ring(q // 2, s // 2, half) + 2 * (q % 2 != s % 2), q))
        pairing = dict(zip(away, reversed(near)))
        owner.append([pairing[k] for k in range(side)])
    return owner


def body(start_block, center, half_width, matrix_tiles, tile_row, tile_col, tile_live):
    vectors, width = start_block.shape
    slots_here = tile_row.shape[1]
    row_count, col_count = lax.axis_size("row"), lax.axis_size("col")
    side = row_count
    core = lax.axis_index("col") % 2
    diagonal = lax.axis_index("row") == lax.axis_index("col") // 2
    axes = ("row", "col")
    owner = column_owner(side)

    def device(r, c2, h):
        return r * col_count + 2 * c2 + h

    span = range(side)
    swap = [(device(r, c2, h), device(r, c2, 1 - h)) for r in span for c2 in span for h in range(2)]
    along_row = [[[device(s, k, h) for k in span] for s in span] for h in range(2)]
    along_col = [[[device(owner[s][k], s, h) for k in span] for s in span] for h in range(2)]
    gather_groups = [along_row[h] + along_col[1 - h] for h in range(2)]
    turns = [
        [pair for s in span for k in span for a, b in [(along_row[h][s][k], along_col[1 - h][s][k])] for pair in ((a, b), (b, a))]
        for h in range(2)
    ]

    def exchange(value, groups):
        return lax.all_to_all(value, axes, 0, 0, axis_index_groups=groups, tiled=False)

    def send(value, pairs):
        return lax.ppermute(value, axes, pairs)

    panel = 2 * side
    ids = jnp.stack([tile_row[0], tile_col[0] + core * panel, tile_live[0]])
    theirs, ids_there = send(start_block, swap), send(ids, swap)
    by_row = jnp.where(core == 0, jnp.stack([start_block, theirs]), jnp.stack([theirs, start_block]))
    own, by_row, ids_there = lax.optimization_barrier((matrix_tiles[0], by_row, ids_there))
    to_column = [pair for s in span for k in span for pair in [(device(s, k, 1), along_col[1][s][k])]]
    start_turned = send(by_row, to_column + [(device(s, k, 0), device(s, k, 0)) for s in span for k in span])
    tiles = keep(own, send(own, swap))

    ids = jnp.concatenate([ids, ids_there], 1)
    alive = ids[2] > 0
    position = jnp.cumsum(alive.astype(jnp.int32)) - 1
    places = 2 * slots_here + GROUP
    hit = (position[None, :] == jnp.arange(places)[:, None]) & alive[None, :]
    count = jnp.sum(alive.astype(jnp.int32))

    def pick(value, empty):
        found = jnp.sum(jnp.where(hit, value[None, :], 0), axis=1)
        return jnp.where(jnp.arange(places) < count, found, empty).astype(jnp.int32)

    slots = pick(jnp.arange(2 * slots_here), 0)
    rows, cols = pick(ids[0], 4 * side), pick(ids[1], 4 * side)

    def table_of(role):
        head = jnp.pad(jnp.stack([role, (count + GROUP - 1) // GROUP]).astype(jnp.int32), (0, places - 2))
        first = role == 0
        return jnp.stack([head, slots, jnp.where(first, rows, cols), jnp.where(first, cols, rows)])

    center_value, half_value = center[0], half_width[0]
    folds = [jnp.full((8, 128), jnp.where(diagonal & (core == h), -center_value, 0.0)) for h in range(2)]
    tables = [table_of(core), table_of(1 - core)]

    start_turned, tiles, tables, folds = lax.optimization_barrier((start_turned, tiles, tables, folds))
    current = start_turned
    earlier = current
    for degree in range(DEG):
        lead = degree % 2
        rounded = current.astype(jnp.bfloat16)
        x = exchange(jnp.broadcast_to(rounded[None], (side, *rounded.shape)), gather_groups[lead])
        partial = products(tables[lead], folds[lead], x.reshape(2 * side, vectors, width), tiles)
        parts = exchange(partial.reshape(side, 2, vectors, width), gather_groups[1 - lead])
        share = jnp.sum(parts.astype(jnp.float32), axis=0)
        product = share + send(share.astype(jnp.bfloat16), turns[1 - lead]).astype(jnp.float32)
        following = product / half_value if degree == 0 else 2.0 * product / half_value - earlier
        earlier, current = current, following

    got = send(jnp.where(core == 0, current[1], earlier[0]), swap)
    return jnp.where(core == 0, current[0], got), jnp.where(core == 0, got, earlier[1])


def solution(mesh):
    in_specs = (
        P(None, ("row", "col")),
        P(),
        P(),
        P("row", "col", None, None),
        P("row", "col"),
        P("row", "col"),
        P("row", "col"),
    )
    out_specs = (P(None, ("row", "col")), P(None, ("row", "col")))
    return jax.shard_map(body, mesh=mesh, in_specs=in_specs, out_specs=out_specs, check_vma=False)
```

```python
import jax
import jax.numpy as jnp
from jax import lax
from jax.experimental import pallas as pl
from jax.experimental.pallas import tpu as pltpu
from jax.sharding import PartitionSpec as P

DEG = 8
GROUP = 24
REST = 4


def keep_kernel(own_ref, other_ref, kept_ref, sems):
    count = own_ref.shape[0]
    copies = [
        pltpu.make_async_copy(ref, kept_ref.at[pl.ds(part * count, count)], sems.at[part])
        for part, ref in enumerate((own_ref, other_ref))
    ]
    for copy in copies:
        copy.start()
    for copy in copies:
        copy.wait()


def keep(own, other):
    count, size, _ = own.shape
    any_space = pl.BlockSpec(memory_space=pl.ANY)
    return pl.pallas_call(
        keep_kernel,
        out_shape=jax.ShapeDtypeStruct((2 * count, size, size), own.dtype),
        in_specs=[any_space, any_space],
        out_specs=pl.BlockSpec(memory_space=pltpu.VMEM),
        scratch_shapes=[pltpu.SemaphoreType.DMA((2,))],
        compiler_params=pltpu.CompilerParams(vmem_limit_bytes=16 * 1024 * 1024),
        cost_estimate=pl.CostEstimate(flops=0, bytes_accessed=4 * count * size * size * 2, transcendentals=0),
    )(own, other)


def products_kernel(table, fold_ref, x_ref, tiles_ref, out_ref, x_wide, total):
    vectors, size = x_wide.shape[1], tiles_ref.shape[-1]
    pairs = x_ref.shape[0]
    low = lax.broadcasted_iota(jnp.int32, (vectors, 128), 1) < 64
    fold = fold_ref[:1, :]

    def place(cluster, half, value):
        x_wide[cluster, :, 128 * half : 128 * (half + 1)] = value.astype(jnp.bfloat16)
        total[cluster, :, 128 * half : 128 * (half + 1)] = value * fold

    for pair in range(pairs):
        first, middle, last = (x_ref[pair, :, 128 * i : 128 * (i + 1)].astype(jnp.float32) for i in range(3))
        middle_rolled, last_rolled = pltpu.roll(middle, 64, 1), pltpu.roll(last, 64, 1)
        place(2 * pair, 0, first)
        place(2 * pair, 1, middle)
        place(2 * pair + 1, 0, jnp.where(low, middle_rolled, last_rolled))
        place(2 * pair + 1, 1, last_rolled)
    for half in range(2):
        place(2 * pairs, half, jnp.zeros((vectors, 128), jnp.float32))

    def run(contract):
        def add(start, members):
            sums = [
                lax.dot_general(
                    x_wide[table[2, start + member], :, :size],
                    tiles_ref[table[1, start + member]],
                    (((1,), (contract,)), ((), ())),
                    preferred_element_type=jnp.float32,
                )
                for member in range(members)
            ]
            for member in range(members):
                total[table[3, start + member], :, :size] += sums[member]

        @pl.loop(0, table[0, 1])
        def _(group):
            add(group * GROUP, GROUP)

        @pl.loop(0, table[0, 2])
        def _(group):
            add(table[0, 1] * GROUP + group * REST, REST)

    @pl.when(table[0, 0] == 0)
    def _():
        run(0)

    @pl.when(table[0, 0] == 1)
    def _():
        run(1)

    for pair in range(pairs):
        even_a, even_b = total[2 * pair, :, :128], total[2 * pair, :, 128:]
        odd_a = pltpu.roll(total[2 * pair + 1, :, :128], 64, 1)
        odd_b = pltpu.roll(total[2 * pair + 1, :, 128:], 64, 1)
        out_ref[pair, :, :128] = even_a.astype(jnp.bfloat16)
        out_ref[pair, :, 128:256] = jnp.where(low, even_b, odd_a).astype(jnp.bfloat16)
        out_ref[pair, :, 256:] = jnp.where(low, odd_a, odd_b).astype(jnp.bfloat16)


def products(table, fold, x, tiles):
    pairs, vectors, width = x.shape
    count, size, _ = tiles.shape
    vmem = pl.BlockSpec(memory_space=pltpu.VMEM)
    return pl.pallas_call(
        products_kernel,
        out_shape=jax.ShapeDtypeStruct(x.shape, jnp.bfloat16),
        in_specs=[pl.BlockSpec(memory_space=pltpu.SMEM), vmem, vmem, vmem],
        out_specs=vmem,
        scratch_shapes=[
            pltpu.VMEM((2 * pairs + 1, vectors, 256), jnp.bfloat16),
            pltpu.VMEM((2 * pairs + 1, vectors, 256), jnp.float32),
        ],
        compiler_params=pltpu.CompilerParams(vmem_limit_bytes=16 * 1024 * 1024),
        cost_estimate=pl.CostEstimate(
            flops=2 * count * size * size * vectors, bytes_accessed=count * size * size * 2, transcendentals=0
        ),
    )(table, fold, x, tiles)


def column_owner(side):
    ring = side // 2

    def place(s, k):
        step = (k - s) % ring
        return 2 * ((s // 2 + ring // 2 - step) % ring) + ((s % 2) ^ (k // ring) ^ (s // ring))

    return [[place(s, k) for k in range(side)] for s in range(side)]


def body(start_block, center, half_width, matrix_tiles, tile_row, tile_col, tile_live):
    vectors, width = start_block.shape
    slots_here = tile_row.shape[1]
    row_count, col_count = lax.axis_size("row"), lax.axis_size("col")
    side = row_count
    core = lax.axis_index("col") % 2
    diagonal = lax.axis_index("row") == lax.axis_index("col") // 2
    axes = ("row", "col")
    owner = column_owner(side)

    def device(r, c2, h):
        return r * col_count + 2 * c2 + h

    span = range(side)
    swap = [(device(r, c2, h), device(r, c2, 1 - h)) for r in span for c2 in span for h in range(2)]
    along_row = [[[device(s, k, h) for k in span] for s in span] for h in range(2)]
    along_col = [[[device(owner[s][k], s, h) for k in span] for s in span] for h in range(2)]
    gather_groups = [along_row[h] + along_col[1 - h] for h in range(2)]
    turns = [
        [pair for s in span for k in span for a, b in [(along_row[h][s][k], along_col[1 - h][s][k])] for pair in ((a, b), (b, a))]
        for h in range(2)
    ]

    def exchange(value, groups):
        return lax.all_to_all(value, axes, 0, 0, axis_index_groups=groups, tiled=False)

    def send(value, pairs):
        return lax.ppermute(value, axes, pairs)

    panel = 2 * side
    ids = jnp.stack([tile_row[0], tile_col[0] + core * panel, tile_live[0]])
    theirs, ids_there = send(start_block, swap), send(ids, swap)
    by_row = jnp.where(core == 0, jnp.stack([start_block, theirs]), jnp.stack([theirs, start_block]))
    own, by_row, ids_there = lax.optimization_barrier((matrix_tiles[0], by_row, ids_there))
    to_column = [pair for s in span for k in span for pair in [(device(s, k, 1), along_col[1][s][k])]]
    start_turned = send(by_row, to_column + [(device(s, k, 0), device(s, k, 0)) for s in span for k in span])
    tiles = keep(own, send(own, swap))

    ids = jnp.concatenate([ids, ids_there], 1)
    alive = ids[2] > 0
    position = jnp.cumsum(alive.astype(jnp.int32)) - 1
    places = 2 * slots_here + REST
    hit = (position[None, :] == jnp.arange(places)[:, None]) & alive[None, :]
    count = jnp.sum(alive.astype(jnp.int32))

    def pick(value, empty):
        found = jnp.sum(jnp.where(hit, value[None, :], 0), axis=1)
        return jnp.where(jnp.arange(places) < count, found, empty).astype(jnp.int32)

    slots = pick(jnp.arange(2 * slots_here), 0)
    rows, cols = pick(ids[0], 4 * side), pick(ids[1], 4 * side)

    def table_of(role):
        rest = (count % GROUP + REST - 1) // REST
        head = jnp.pad(jnp.stack([role, count // GROUP, rest]).astype(jnp.int32), (0, places - 3))
        first = role == 0
        return jnp.stack([head, slots, jnp.where(first, rows, cols), jnp.where(first, cols, rows)])

    center_value, half_value = center[0], half_width[0]
    fold = jnp.full((8, 128), jnp.where(diagonal, -0.5 * center_value, 0.0))
    tables = [table_of(core), table_of(1 - core)]

    start_turned, tiles, tables, fold = lax.optimization_barrier((start_turned, tiles, tables, fold))
    current = start_turned
    earlier = current
    for degree in range(DEG):
        lead = degree % 2
        rounded = current.astype(jnp.bfloat16)
        x = exchange(jnp.broadcast_to(rounded[None], (side, *rounded.shape)), gather_groups[lead])
        partial = products(tables[lead], fold, x.reshape(2 * side, vectors, width), tiles)
        parts = exchange(partial.reshape(side, 2, vectors, width), gather_groups[1 - lead])
        share = jnp.sum(parts.astype(jnp.float32), axis=0)
        product = share + send(share.astype(jnp.bfloat16), turns[1 - lead]).astype(jnp.float32)
        following = product / half_value if degree == 0 else 2.0 * product / half_value - earlier
        earlier, current = current, following

    got = send(jnp.where(core == 0, current[1], earlier[0]), swap)
    return jnp.where(core == 0, current[0], got), jnp.where(core == 0, got, earlier[1])


def solution(mesh):
    in_specs = (
        P(None, ("row", "col")),
        P(),
        P(),
        P("row", "col", None, None),
        P("row", "col"),
        P("row", "col"),
        P("row", "col"),
    )
    out_specs = (P(None, ("row", "col")), P(None, ("row", "col")))
    return jax.shard_map(body, mesh=mesh, in_specs=in_specs, out_specs=out_specs, check_vma=False)
```

```python
import jax
import jax.numpy as jnp
from jax import lax
from jax.experimental import pallas as pl
from jax.experimental.pallas import tpu as pltpu
from jax.sharding import PartitionSpec as P

DEG = 8
GROUP = 24
REST = 4


def keep_kernel(own_ref, other_ref, kept_ref, sems):
    count = own_ref.shape[0]
    copies = [
        pltpu.make_async_copy(ref, kept_ref.at[pl.ds(part * count, count)], sems.at[part])
        for part, ref in enumerate((own_ref, other_ref))
    ]
    for copy in copies:
        copy.start()
    for copy in copies:
        copy.wait()


def keep(own, other):
    count, size, _ = own.shape
    any_space = pl.BlockSpec(memory_space=pl.ANY)
    return pl.pallas_call(
        keep_kernel,
        out_shape=jax.ShapeDtypeStruct((2 * count, size, size), own.dtype),
        in_specs=[any_space, any_space],
        out_specs=pl.BlockSpec(memory_space=pltpu.VMEM),
        scratch_shapes=[pltpu.SemaphoreType.DMA((2,))],
        compiler_params=pltpu.CompilerParams(vmem_limit_bytes=16 * 1024 * 1024),
        cost_estimate=pl.CostEstimate(flops=0, bytes_accessed=4 * count * size * size * 2, transcendentals=0),
    )(own, other)


def products_kernel(table, fold_ref, x_ref, tiles_ref, out_ref, x_wide, total):
    vectors, size = x_wide.shape[1], tiles_ref.shape[-1]
    pairs = x_ref.shape[0]
    low = lax.broadcasted_iota(jnp.int32, (vectors, 128), 1) < 64
    fold = fold_ref[:1, :]

    def place(cluster, half, value):
        x_wide[cluster, :, 128 * half : 128 * (half + 1)] = value.astype(jnp.bfloat16)
        total[cluster, :, 128 * half : 128 * (half + 1)] = value * fold

    for pair in range(pairs):
        first, middle, last = (x_ref[pair, :, 128 * i : 128 * (i + 1)].astype(jnp.float32) for i in range(3))
        middle_rolled, last_rolled = pltpu.roll(middle, 64, 1), pltpu.roll(last, 64, 1)
        place(2 * pair, 0, first)
        place(2 * pair, 1, middle)
        place(2 * pair + 1, 0, jnp.where(low, middle_rolled, last_rolled))
        place(2 * pair + 1, 1, last_rolled)
    for half in range(2):
        place(2 * pairs, half, jnp.zeros((vectors, 128), jnp.float32))

    def run(contract):
        def add(start, members):
            sums = [
                lax.dot_general(
                    x_wide[table[2, start + member], :, :size],
                    tiles_ref[table[1, start + member]],
                    (((1,), (contract,)), ((), ())),
                    preferred_element_type=jnp.float32,
                )
                for member in range(members)
            ]
            for member in range(members):
                total[table[3, start + member], :, :size] += sums[member]

        @pl.loop(0, table[0, 1])
        def _(group):
            add(group * GROUP, GROUP)

        @pl.loop(0, table[0, 2])
        def _(group):
            add(table[0, 1] * GROUP + group * REST, REST)

    @pl.when(table[0, 0] == 0)
    def _():
        run(0)

    @pl.when(table[0, 0] == 1)
    def _():
        run(1)

    for pair in range(pairs):
        even_a, even_b = total[2 * pair, :, :128], total[2 * pair, :, 128:]
        odd_a = pltpu.roll(total[2 * pair + 1, :, :128], 64, 1)
        odd_b = pltpu.roll(total[2 * pair + 1, :, 128:], 64, 1)
        out_ref[pair, :, :128] = even_a.astype(jnp.bfloat16)
        out_ref[pair, :, 128:256] = jnp.where(low, even_b, odd_a).astype(jnp.bfloat16)
        out_ref[pair, :, 256:] = jnp.where(low, odd_a, odd_b).astype(jnp.bfloat16)


def products(table, fold, x, tiles):
    pairs, vectors, width = x.shape
    count, size, _ = tiles.shape
    vmem = pl.BlockSpec(memory_space=pltpu.VMEM)
    return pl.pallas_call(
        products_kernel,
        out_shape=jax.ShapeDtypeStruct(x.shape, jnp.bfloat16),
        in_specs=[pl.BlockSpec(memory_space=pltpu.SMEM), vmem, vmem, vmem],
        out_specs=vmem,
        scratch_shapes=[
            pltpu.VMEM((2 * pairs + 1, vectors, 256), jnp.bfloat16),
            pltpu.VMEM((2 * pairs + 1, vectors, 256), jnp.float32),
        ],
        compiler_params=pltpu.CompilerParams(vmem_limit_bytes=16 * 1024 * 1024),
        cost_estimate=pl.CostEstimate(
            flops=2 * count * size * size * vectors, bytes_accessed=count * size * size * 2, transcendentals=0
        ),
    )(table, fold, x, tiles)


def column_owner(side):
    ring = side // 2

    def place(s, k):
        step = (k - s) % ring
        return 2 * ((s // 2 + ring // 2 - step) % ring) + ((s % 2) ^ (k // ring) ^ (s // ring))

    return [[place(s, k) for k in range(side)] for s in range(side)]


def body(start_block, center, half_width, matrix_tiles, tile_row, tile_col, tile_live):
    vectors, width = start_block.shape
    slots_here = tile_row.shape[1]
    row_count, col_count = lax.axis_size("row"), lax.axis_size("col")
    side = row_count
    core = lax.axis_index("col") % 2
    diagonal = lax.axis_index("row") == lax.axis_index("col") // 2
    axes = ("row", "col")
    owner = column_owner(side)

    def device(r, c2, h):
        return r * col_count + 2 * c2 + h

    span = range(side)
    swap = [(device(r, c2, h), device(r, c2, 1 - h)) for r in span for c2 in span for h in range(2)]
    along_row = [[[device(s, k, h) for k in span] for s in span] for h in range(2)]
    along_col = [[[device(owner[s][k], s, h) for k in span] for s in span] for h in range(2)]
    gather_groups = [along_row[h] + along_col[1 - h] for h in range(2)]
    turns = [
        [pair for s in span for k in span for a, b in [(along_row[h][s][k], along_col[1 - h][s][k])] for pair in ((a, b), (b, a))]
        for h in range(2)
    ]

    def exchange(value, groups):
        return lax.all_to_all(value, axes, 0, 0, axis_index_groups=groups, tiled=False)

    def send(value, pairs):
        return lax.ppermute(value, axes, pairs)

    panel = 2 * side
    ids = jnp.stack([tile_row[0], tile_col[0] + core * panel, tile_live[0]])
    theirs, ids_there = send(start_block, swap), send(ids, swap)
    by_row = jnp.where(core == 0, jnp.stack([start_block, theirs]), jnp.stack([theirs, start_block]))
    to_column = [pair for s in span for k in span for pair in [(device(s, k, 1), along_col[1][s][k])]]
    start_turned = send(by_row, to_column + [(device(s, k, 0), device(s, k, 0)) for s in span for k in span])

    by_row, ids_there, own = lax.optimization_barrier((by_row, ids_there, matrix_tiles[0]))
    other = send(own, swap)
    ids = jnp.concatenate([ids, ids_there], 1)
    alive = ids[2] > 0
    order = jnp.arange(2 * slots_here)
    position = jnp.sum(jnp.where((order[None, :] < order[:, None]) & alive[None, :], 1, 0), axis=1)
    places = 2 * slots_here + REST
    hit = (position[None, :] == jnp.arange(places)[:, None]) & alive[None, :]
    count = jnp.sum(alive.astype(jnp.int32))

    def pick(value, empty):
        found = jnp.sum(jnp.where(hit, value[None, :], 0), axis=1)
        return jnp.where(jnp.arange(places) < count, found, empty).astype(jnp.int32)

    slots = pick(jnp.arange(2 * slots_here), 0)
    rows, cols = pick(ids[0], 4 * side), pick(ids[1], 4 * side)

    def table_of(role):
        rest = (count % GROUP + REST - 1) // REST
        head = jnp.pad(jnp.stack([role, count // GROUP, rest]).astype(jnp.int32), (0, places - 3))
        first = role == 0
        return jnp.stack([head, slots, jnp.where(first, rows, cols), jnp.where(first, cols, rows)])

    center_value, half_value = center[0], half_width[0]
    fold = jnp.full((8, 128), jnp.where(diagonal, -0.5 * center_value, 0.0))
    tables = [table_of(core), table_of(1 - core)]

    start_turned, tables, fold = lax.optimization_barrier((start_turned, tables, fold))
    current = start_turned
    earlier = current
    for degree in range(DEG):
        lead = degree % 2
        rounded = current.astype(jnp.bfloat16)
        x = exchange(jnp.broadcast_to(rounded[None], (side, *rounded.shape)), gather_groups[lead])
        if degree == 0:
            x, own, other = lax.optimization_barrier((x, own, other))
            tiles = keep(own, other)
        partial = products(tables[lead], fold, x.reshape(2 * side, vectors, width), tiles)
        parts = exchange(partial.reshape(side, 2, vectors, width), gather_groups[1 - lead])
        share = jnp.sum(parts.astype(jnp.float32), axis=0)
        product = share + send(share.astype(jnp.bfloat16), turns[1 - lead]).astype(jnp.float32)
        following = product / half_value if degree == 0 else 2.0 * product / half_value - earlier
        earlier, current = current, following

    got = send(jnp.where(core == 0, current[1], earlier[0]), swap)
    return jnp.where(core == 0, current[0], got), jnp.where(core == 0, got, earlier[1])


def solution(mesh):
    in_specs = (
        P(None, ("row", "col")),
        P(),
        P(),
        P("row", "col", None, None),
        P("row", "col"),
        P("row", "col"),
        P("row", "col"),
    )
    out_specs = (P(None, ("row", "col")), P(None, ("row", "col")))
    return jax.shard_map(body, mesh=mesh, in_specs=in_specs, out_specs=out_specs, check_vma=False)
```

```python
import jax
import jax.numpy as jnp
from jax import lax
from jax.experimental import pallas as pl
from jax.experimental.pallas import tpu as pltpu
from jax.sharding import PartitionSpec as P

DEG = 8
GROUP = 32
REST = 8


def keep_kernel(own_ref, other_ref, kept_ref, sems):
    count = own_ref.shape[0]
    copies = [
        pltpu.make_async_copy(ref, kept_ref.at[pl.ds(part * count, count)], sems.at[part])
        for part, ref in enumerate((own_ref, other_ref))
    ]
    for copy in copies:
        copy.start()
    for copy in copies:
        copy.wait()


def keep(own, other):
    count, size, _ = own.shape
    any_space = pl.BlockSpec(memory_space=pl.ANY)
    return pl.pallas_call(
        keep_kernel,
        out_shape=jax.ShapeDtypeStruct((2 * count, size, size), own.dtype),
        in_specs=[any_space, any_space],
        out_specs=pl.BlockSpec(memory_space=pltpu.VMEM),
        scratch_shapes=[pltpu.SemaphoreType.DMA((2,))],
        compiler_params=pltpu.CompilerParams(vmem_limit_bytes=16 * 1024 * 1024),
        cost_estimate=pl.CostEstimate(flops=0, bytes_accessed=4 * count * size * size * 2, transcendentals=0),
    )(own, other)


def products_kernel(table_ref, fold_ref, x_ref, tiles_ref, out_ref, x_wide, total, table, sem):
    vectors, size = x_wide.shape[1], tiles_ref.shape[-1]
    pairs = x_ref.shape[0]
    low = lax.broadcasted_iota(jnp.int32, (vectors, 128), 1) < 64
    fold = fold_ref[:1, :]
    fetch = pltpu.make_async_copy(table_ref, table, sem)
    fetch.start()

    def place(cluster, half, value):
        x_wide[cluster, :, 128 * half : 128 * (half + 1)] = value.astype(jnp.bfloat16)
        total[cluster, :, 128 * half : 128 * (half + 1)] = value * fold

    for pair in range(pairs):
        first, middle, last = (x_ref[pair, :, 128 * i : 128 * (i + 1)].astype(jnp.float32) for i in range(3))
        middle_rolled, last_rolled = pltpu.roll(middle, 64, 1), pltpu.roll(last, 64, 1)
        place(2 * pair, 0, first)
        place(2 * pair, 1, middle)
        place(2 * pair + 1, 0, jnp.where(low, middle_rolled, last_rolled))
        place(2 * pair + 1, 1, last_rolled)
    for half in range(2):
        place(2 * pairs, half, jnp.zeros((vectors, 128), jnp.float32))

    fetch.wait()

    def run(contract):
        def add(start, members):
            sums = [
                lax.dot_general(
                    x_wide[table[2, start + member], :, :size],
                    tiles_ref[table[1, start + member]],
                    (((1,), (contract,)), ((), ())),
                    preferred_element_type=jnp.float32,
                )
                for member in range(members)
            ]
            for member in range(members):
                total[table[3, start + member], :, :size] += sums[member]

        @pl.loop(0, table[0, 1])
        def _(group):
            add(group * GROUP, GROUP)

        @pl.loop(0, table[0, 2])
        def _(group):
            add(table[0, 1] * GROUP + group * REST, REST)

    @pl.when(table[0, 0] == 0)
    def _():
        run(0)

    @pl.when(table[0, 0] == 1)
    def _():
        run(1)

    for pair in range(pairs):
        even_a, even_b = total[2 * pair, :, :128], total[2 * pair, :, 128:]
        odd_a = pltpu.roll(total[2 * pair + 1, :, :128], 64, 1)
        odd_b = pltpu.roll(total[2 * pair + 1, :, 128:], 64, 1)
        out_ref[pair, :, :128] = even_a.astype(jnp.bfloat16)
        out_ref[pair, :, 128:256] = jnp.where(low, even_b, odd_a).astype(jnp.bfloat16)
        out_ref[pair, :, 256:] = jnp.where(low, odd_a, odd_b).astype(jnp.bfloat16)


def products(table, fold, x, tiles):
    pairs, vectors, width = x.shape
    count, size, _ = tiles.shape
    vmem = pl.BlockSpec(memory_space=pltpu.VMEM)
    return pl.pallas_call(
        products_kernel,
        out_shape=jax.ShapeDtypeStruct(x.shape, jnp.bfloat16),
        in_specs=[pl.BlockSpec(memory_space=pl.ANY), vmem, vmem, vmem],
        out_specs=vmem,
        scratch_shapes=[
            pltpu.VMEM((2 * pairs + 1, vectors, 256), jnp.bfloat16),
            pltpu.VMEM((2 * pairs + 1, vectors, 256), jnp.float32),
            pltpu.SMEM(table.shape, jnp.int32),
            pltpu.SemaphoreType.DMA,
        ],
        compiler_params=pltpu.CompilerParams(vmem_limit_bytes=16 * 1024 * 1024),
        cost_estimate=pl.CostEstimate(
            flops=2 * count * size * size * vectors, bytes_accessed=count * size * size * 2, transcendentals=0
        ),
    )(table, fold, x, tiles)


def column_owner(side):
    ring = side // 2

    def place(s, k):
        step = (k - s) % ring
        return 2 * ((s // 2 + ring // 2 - step) % ring) + ((s % 2) ^ (k // ring) ^ (s // ring))

    return [[place(s, k) for k in range(side)] for s in range(side)]


def body(start_block, center, half_width, matrix_tiles, tile_row, tile_col, tile_live):
    vectors, width = start_block.shape
    slots_here = tile_row.shape[1]
    row_count, col_count = lax.axis_size("row"), lax.axis_size("col")
    side = row_count
    core = lax.axis_index("col") % 2
    diagonal = lax.axis_index("row") == lax.axis_index("col") // 2
    axes = ("row", "col")
    owner = column_owner(side)

    def device(r, c2, h):
        return r * col_count + 2 * c2 + h

    span = range(side)
    swap = [(device(r, c2, h), device(r, c2, 1 - h)) for r in span for c2 in span for h in range(2)]
    along_row = [[[device(s, k, h) for k in span] for s in span] for h in range(2)]
    along_col = [[[device(owner[s][k], s, h) for k in span] for s in span] for h in range(2)]
    gather_groups = [along_row[h] + along_col[1 - h] for h in range(2)]
    turns = [
        [pair for s in span for k in span for a, b in [(along_row[h][s][k], along_col[1 - h][s][k])] for pair in ((a, b), (b, a))]
        for h in range(2)
    ]

    def exchange(value, groups):
        return lax.all_to_all(value, axes, 0, 0, axis_index_groups=groups, tiled=False)

    def send(value, pairs):
        return lax.ppermute(value, axes, pairs)

    panel = 2 * side
    ids = jnp.stack([tile_row[0], tile_col[0] + core * panel, tile_live[0]])
    theirs, ids_there = send(start_block, swap), send(ids, swap)
    by_row = jnp.where(core == 0, jnp.stack([start_block, theirs]), jnp.stack([theirs, start_block]))
    to_column = [pair for s in span for k in span for pair in [(device(s, k, 1), along_col[1][s][k])]]
    start_turned = send(by_row, to_column + [(device(s, k, 0), device(s, k, 0)) for s in span for k in span])

    by_row, ids_there, own = lax.optimization_barrier((by_row, ids_there, matrix_tiles[0]))
    other = send(own, swap)
    ids = jnp.concatenate([ids, ids_there], 1)
    alive = ids[2] > 0
    order = jnp.arange(2 * slots_here)
    position = jnp.sum(jnp.where((order[None, :] < order[:, None]) & alive[None, :], 1, 0), axis=1)
    places = 2 * slots_here + REST
    hit = (position[None, :] == jnp.arange(places)[:, None]) & alive[None, :]
    count = jnp.sum(alive.astype(jnp.int32))

    def pick(value, empty):
        found = jnp.sum(jnp.where(hit, value[None, :], 0), axis=1)
        return jnp.where(jnp.arange(places) < count, found, empty).astype(jnp.int32)

    slots = pick(jnp.arange(2 * slots_here), 0)
    rows, cols = pick(ids[0], 4 * side), pick(ids[1], 4 * side)

    def table_of(role):
        rest = (count % GROUP + REST - 1) // REST
        head = jnp.pad(jnp.stack([role, count // GROUP, rest]).astype(jnp.int32), (0, places - 3))
        first = role == 0
        return jnp.stack([head, slots, jnp.where(first, rows, cols), jnp.where(first, cols, rows)])

    center_value, half_value = center[0], half_width[0]
    fold = jnp.full((8, 128), jnp.where(diagonal, -0.5 * center_value, 0.0))
    tables = [table_of(core), table_of(1 - core)]

    start_turned, tables, fold = lax.optimization_barrier((start_turned, tables, fold))
    current = start_turned
    earlier = current
    for degree in range(DEG):
        lead = degree % 2
        rounded = current.astype(jnp.bfloat16)
        x = exchange(jnp.broadcast_to(rounded[None], (side, *rounded.shape)), gather_groups[lead])
        if degree == 0:
            x, own, other = lax.optimization_barrier((x, own, other))
            tiles = keep(own, other)
        partial = products(tables[lead], fold, x.reshape(2 * side, vectors, width), tiles)
        parts = exchange(partial.reshape(side, 2, vectors, width), gather_groups[1 - lead])
        share = jnp.sum(parts.astype(jnp.float32), axis=0)
        product = share + send(share.astype(jnp.bfloat16), turns[1 - lead]).astype(jnp.float32)
        following = product / half_value if degree == 0 else 2.0 * product / half_value - earlier
        earlier, current = current, following

    got = send(jnp.where(core == 0, current[1], earlier[0]), swap)
    return jnp.where(core == 0, current[0], got), jnp.where(core == 0, got, earlier[1])


def solution(mesh):
    in_specs = (
        P(None, ("row", "col")),
        P(),
        P(),
        P("row", "col", None, None),
        P("row", "col"),
        P("row", "col"),
        P("row", "col"),
    )
    out_specs = (P(None, ("row", "col")), P(None, ("row", "col")))
    return jax.shard_map(body, mesh=mesh, in_specs=in_specs, out_specs=out_specs, check_vma=False)
```

```python
import jax
import jax.numpy as jnp
from jax import lax
from jax.experimental import pallas as pl
from jax.experimental.pallas import tpu as pltpu
from jax.sharding import PartitionSpec as P

DEG = 8
GROUP = 32
REST = 16


def keep_kernel(own_ref, other_ref, kept_ref, sems):
    count = own_ref.shape[0]
    copies = [
        pltpu.make_async_copy(ref, kept_ref.at[pl.ds(part * count, count)], sems.at[part])
        for part, ref in enumerate((own_ref, other_ref))
    ]
    for copy in copies:
        copy.start()
    for copy in copies:
        copy.wait()


def keep(own, other):
    count, size, _ = own.shape
    any_space = pl.BlockSpec(memory_space=pl.ANY)
    return pl.pallas_call(
        keep_kernel,
        out_shape=jax.ShapeDtypeStruct((2 * count, size, size), own.dtype),
        in_specs=[any_space, any_space],
        out_specs=pl.BlockSpec(memory_space=pltpu.VMEM),
        scratch_shapes=[pltpu.SemaphoreType.DMA((2,))],
        compiler_params=pltpu.CompilerParams(vmem_limit_bytes=16 * 1024 * 1024),
        cost_estimate=pl.CostEstimate(flops=0, bytes_accessed=4 * count * size * size * 2, transcendentals=0),
    )(own, other)


def products_kernel(table_ref, fold_ref, x_ref, tiles_ref, out_ref, x_wide, total, table, sem):
    vectors, size = x_wide.shape[1], tiles_ref.shape[-1]
    pairs = x_ref.shape[0]
    low = lax.broadcasted_iota(jnp.int32, (vectors, 128), 1) < 64
    fold = fold_ref[:1, :]
    fetch = pltpu.make_async_copy(table_ref, table, sem)
    fetch.start()

    def place(cluster, half, value):
        x_wide[cluster, :, 128 * half : 128 * (half + 1)] = value.astype(jnp.bfloat16)
        total[cluster, :, 128 * half : 128 * (half + 1)] = value * fold

    for pair in range(pairs):
        first, middle, last = (x_ref[pair, :, 128 * i : 128 * (i + 1)].astype(jnp.float32) for i in range(3))
        middle_rolled, last_rolled = pltpu.roll(middle, 64, 1), pltpu.roll(last, 64, 1)
        place(2 * pair, 0, first)
        place(2 * pair, 1, middle)
        place(2 * pair + 1, 0, jnp.where(low, middle_rolled, last_rolled))
        place(2 * pair + 1, 1, last_rolled)
    for half in range(2):
        place(2 * pairs, half, jnp.zeros((vectors, 128), jnp.float32))

    fetch.wait()

    def run(contract):
        def add(start, members):
            sums = [
                lax.dot_general(
                    x_wide[table[2, start + member], :, :size],
                    tiles_ref[table[1, start + member]],
                    (((1,), (contract,)), ((), ())),
                    preferred_element_type=jnp.float32,
                )
                for member in range(members)
            ]
            for member in range(members):
                total[table[3, start + member], :, :size] += sums[member]

        @pl.loop(0, table[0, 1])
        def _(group):
            add(group * GROUP, GROUP)

        @pl.loop(0, table[0, 2])
        def _(group):
            add(table[0, 1] * GROUP + group * REST, REST)

    @pl.when(table[0, 0] == 0)
    def _():
        run(0)

    @pl.when(table[0, 0] == 1)
    def _():
        run(1)

    for pair in range(pairs):
        even_a, even_b = total[2 * pair, :, :128], total[2 * pair, :, 128:]
        odd_a = pltpu.roll(total[2 * pair + 1, :, :128], 64, 1)
        odd_b = pltpu.roll(total[2 * pair + 1, :, 128:], 64, 1)
        out_ref[pair, :, :128] = even_a.astype(jnp.bfloat16)
        out_ref[pair, :, 128:256] = jnp.where(low, even_b, odd_a).astype(jnp.bfloat16)
        out_ref[pair, :, 256:] = jnp.where(low, odd_a, odd_b).astype(jnp.bfloat16)


def products(table, fold, x, tiles):
    pairs, vectors, width = x.shape
    count, size, _ = tiles.shape
    vmem = pl.BlockSpec(memory_space=pltpu.VMEM)
    return pl.pallas_call(
        products_kernel,
        out_shape=jax.ShapeDtypeStruct(x.shape, jnp.bfloat16),
        in_specs=[pl.BlockSpec(memory_space=pl.ANY), vmem, vmem, vmem],
        out_specs=vmem,
        scratch_shapes=[
            pltpu.VMEM((2 * pairs + 1, vectors, 256), jnp.bfloat16),
            pltpu.VMEM((2 * pairs + 1, vectors, 256), jnp.float32),
            pltpu.SMEM(table.shape, jnp.int32),
            pltpu.SemaphoreType.DMA,
        ],
        compiler_params=pltpu.CompilerParams(vmem_limit_bytes=16 * 1024 * 1024),
        cost_estimate=pl.CostEstimate(
            flops=2 * count * size * size * vectors, bytes_accessed=count * size * size * 2, transcendentals=0
        ),
    )(table, fold, x, tiles)


def column_owner(side):
    ring = side // 2

    def place(s, k):
        step = (k - s) % ring
        return 2 * ((s // 2 + ring // 2 - step) % ring) + ((s % 2) ^ (k // ring) ^ (s // ring))

    return [[place(s, k) for k in range(side)] for s in range(side)]


def body(start_block, center, half_width, matrix_tiles, tile_row, tile_col, tile_live):
    vectors, width = start_block.shape
    slots_here = tile_row.shape[1]
    row_count, col_count = lax.axis_size("row"), lax.axis_size("col")
    side = row_count
    core = lax.axis_index("col") % 2
    diagonal = lax.axis_index("row") == lax.axis_index("col") // 2
    axes = ("row", "col")
    owner = column_owner(side)

    def device(r, c2, h):
        return r * col_count + 2 * c2 + h

    span = range(side)
    swap = [(device(r, c2, h), device(r, c2, 1 - h)) for r in span for c2 in span for h in range(2)]
    along_row = [[[device(s, k, h) for k in span] for s in span] for h in range(2)]
    along_col = [[[device(owner[s][k], s, h) for k in span] for s in span] for h in range(2)]
    gather_groups = [along_row[h] + along_col[1 - h] for h in range(2)]
    turns = [
        [pair for s in span for k in span for a, b in [(along_row[h][s][k], along_col[1 - h][s][k])] for pair in ((a, b), (b, a))]
        for h in range(2)
    ]

    def exchange(value, groups):
        return lax.all_to_all(value, axes, 0, 0, axis_index_groups=groups, tiled=False)

    def send(value, pairs):
        return lax.ppermute(value, axes, pairs)

    panel = 2 * side
    ids = jnp.stack([tile_row[0], tile_col[0] + core * panel, tile_live[0]])
    theirs, ids_there = send(start_block, swap), send(ids, swap)
    by_row = jnp.where(core == 0, jnp.stack([start_block, theirs]), jnp.stack([theirs, start_block]))
    to_column = [pair for s in span for k in span for pair in [(device(s, k, 1), along_col[1][s][k])]]
    start_turned = send(by_row, to_column + [(device(s, k, 0), device(s, k, 0)) for s in span for k in span])

    by_row, ids_there, own = lax.optimization_barrier((by_row, ids_there, matrix_tiles[0]))
    other = send(own, swap)
    ids = jnp.concatenate([ids, ids_there], 1)
    alive = ids[2] > 0
    order = jnp.arange(2 * slots_here)
    position = jnp.sum(jnp.where((order[None, :] < order[:, None]) & alive[None, :], 1, 0), axis=1)
    places = 2 * slots_here + REST
    hit = (position[None, :] == jnp.arange(places)[:, None]) & alive[None, :]
    count = jnp.sum(alive.astype(jnp.int32))

    def pick(value, empty):
        found = jnp.sum(jnp.where(hit, value[None, :], 0), axis=1)
        return jnp.where(jnp.arange(places) < count, found, empty).astype(jnp.int32)

    slots = pick(jnp.arange(2 * slots_here), 0)
    rows, cols = pick(ids[0], 4 * side), pick(ids[1], 4 * side)

    def table_of(role):
        rest = (count % GROUP + REST - 1) // REST
        head = jnp.pad(jnp.stack([role, count // GROUP, rest]).astype(jnp.int32), (0, places - 3))
        first = role == 0
        return jnp.stack([head, slots, jnp.where(first, rows, cols), jnp.where(first, cols, rows)])

    center_value, half_value = center[0], half_width[0]
    fold = jnp.full((8, 128), jnp.where(diagonal, -0.5 * center_value, 0.0))
    tables = [table_of(core), table_of(1 - core)]

    start_turned, tables, fold = lax.optimization_barrier((start_turned, tables, fold))
    current = start_turned
    earlier = current
    for degree in range(DEG):
        lead = degree % 2
        rounded = current.astype(jnp.bfloat16)
        x = exchange(jnp.broadcast_to(rounded[None], (side, *rounded.shape)), gather_groups[lead])
        if degree == 0:
            x, own, other = lax.optimization_barrier((x, own, other))
            tiles = keep(own, other)
        partial = products(tables[lead], fold, x.reshape(2 * side, vectors, width), tiles)
        parts = exchange(partial.reshape(side, 2, vectors, width), gather_groups[1 - lead])
        share = jnp.sum(parts.astype(jnp.float32), axis=0)
        product = share + send(share.astype(jnp.bfloat16), turns[1 - lead]).astype(jnp.float32)
        following = product / half_value if degree == 0 else 2.0 * product / half_value - earlier
        earlier, current = current, following

    got = send(jnp.where(core == 0, current[1], earlier[0]), swap)
    return jnp.where(core == 0, current[0], got), jnp.where(core == 0, got, earlier[1])


def solution(mesh):
    in_specs = (
        P(None, ("row", "col")),
        P(),
        P(),
        P("row", "col", None, None),
        P("row", "col"),
        P("row", "col"),
        P("row", "col"),
    )
    out_specs = (P(None, ("row", "col")), P(None, ("row", "col")))
    return jax.shard_map(body, mesh=mesh, in_specs=in_specs, out_specs=out_specs, check_vma=False)
```
